32 devices in a mesh: subj: 2 (over x), vox: 16 (over z, y, core).
Axes of the slice: x: 2, y: 2, z: 4, core: 2. Of those that a mesh axis runs over, the one named last changes fastest.
Arguments:
- data: bfloat16 [2, 450, 16384], P('subj', None, 'vox'), may hold values from -6 to 6
- maps: bfloat16 [2, 256, 16384], P('subj', None, 'vox'), may hold values from -0.046875 to 0.046875
Outputs:
- response: float32 [450, 256], replicated
- new_maps: bfloat16 [2, 256, 16384], P('subj', None, 'vox')
The draws below stay inside these ranges and needn't reach their ends.
All inputs are finite; a program needn't handle non-finite values.
Results may differ from the reference program's by a relative error of at most 0.0043.
The reference program's roundings to bfloat16 on the way count: a program that leaves them out, or rounds other values in their place, can miss the bound.
Values sent between devices are 32-bit elements; how exact they have to be, the bound alone decides.
No kernel may reach another device: no remote copies, remote signals or barrier semaphores. Data moves between devices by JAX's collectives and lax.ppermute only.
A program may use at most 64 MiB of HBM per device.

```python
import jax
import jax.numpy as jnp
from jax import lax

K = 256
TRS = 450
ITERS = 1
NS_STEPS = 5
SUBJECTS = 2
GRAYORDINATE_NUM = 16384


def block_levels(stream_key, shape, pieces, least, high):
    factor_of, own = 1.0, jax.random.fold_in(stream_key, 6)
    for dim, blocks in pieces:
        heights = jnp.exp(jax.random.uniform(jax.random.fold_in(own, dim), (blocks,), jnp.float32, least / len(pieces), high / len(pieces)))
        factor_of = factor_of * jnp.repeat(heights, shape[dim] // blocks).reshape([-1 if axis == dim else 1 for axis in range(len(shape))])
    return factor_of


def gaussian(stream_key, dims, deviation, reach, pieces=(), kind=jnp.bfloat16):
    drawn = jax.random.normal(stream_key, dims, jnp.float32) * deviation
    if len(pieces) > 0:
        drawn = block_levels(stream_key, dims, pieces, -0.22, 0.18) * drawn
    return jnp.clip(drawn, min=-reach, max=reach).astype(kind)


def setup_inputs(seed: int = 0) -> dict:
    streams_of = jax.random.split(jax.random.key(seed), 3)
    return {
        "data": gaussian(streams_of[0], (SUBJECTS, TRS, GRAYORDINATE_NUM), 1.0, 6.0, ((0, 2), (2, 16))),
        "maps": gaussian(streams_of[1], (SUBJECTS, K, GRAYORDINATE_NUM), GRAYORDINATE_NUM ** -0.5, 0.046875, ((0, 2), (2, 16))),
    }


def whiten(gram):
    scale = jnp.sqrt(jnp.sum(gram * gram) + 1e-06)
    present_estimate = gram / scale
    eye = jnp.eye(gram.shape[0], dtype=jnp.float32)
    inverse = eye
    for step in range(NS_STEPS):
        middle = 1.5 * eye - 0.5 * jnp.dot(inverse, present_estimate, precision=lax.Precision.HIGHEST)
        present_estimate = jnp.dot(present_estimate, middle, precision=lax.Precision.HIGHEST)
        inverse = jnp.dot(middle, inverse, precision=lax.Precision.HIGHEST)
    return inverse / jnp.sqrt(scale)

def reference(data, maps):
    present_estimate = [maps[i] for i in range(SUBJECTS)]
    response = jnp.zeros((TRS, K), jnp.float32)
    for it in range(ITERS):
        total = jnp.zeros((TRS, K), jnp.float32)
        for i in range(SUBJECTS):
            total = total + jnp.dot(data[i], present_estimate[i].T, preferred_element_type=jnp.float32)
        response = total / SUBJECTS
        common_signal = response.astype(jnp.bfloat16)
        for i in range(SUBJECTS):
            projected_signal = jnp.dot(common_signal.T, data[i], preferred_element_type=jnp.float32)
            gram = jnp.dot(projected_signal, projected_signal.T, precision=lax.Precision.HIGHEST)
            subject_factor = whiten(gram)
            present_estimate[i] = jnp.dot(subject_factor, projected_signal, precision=lax.Precision.HIGHEST).astype(jnp.bfloat16)
    return (response, jnp.stack(present_estimate))
```

```python
import functools

import jax
import jax.numpy as jnp
from jax import lax
from jax.experimental import pallas as pl
from jax.experimental.pallas import tpu as pltpu
from jax.sharding import PartitionSpec as P

NS_STEPS = 5
VMEM_LIMIT = 40 * 1024 * 1024
AXES = ("subj", "vox")
NT = (((1,), (1,)), ((), ()))


def dot(a, b):
    return jnp.dot(a, b, preferred_element_type=jnp.float32)


def dot_nt(a, b):
    return lax.dot_general(a, b, NT, preferred_element_type=jnp.float32)


def split(a):
    high = a.astype(jnp.bfloat16)
    return high, (a - high.astype(jnp.float32)).astype(jnp.bfloat16)


def dot3(a, b):
    (ah, al), (bh, bl) = split(a), split(b)
    return dot(ah, bh) + (dot(ah, bl) + dot(al, bh))


def grid_of(rows, cols):
    return (
        lax.broadcasted_iota(jnp.int32, (rows, cols), 0),
        lax.broadcasted_iota(jnp.int32, (rows, cols), 1),
    )


def partials_kernel(times, place_ref, data_ref, maps_ref, send_ref, keep_ref, padded):
    full, comps = padded.shape[0], maps_ref.shape[0]
    half, block = comps // 2, full // 2
    tail = times // 16 * 16
    padded[tail:, :] = jnp.zeros((full - tail, padded.shape[1]), padded.dtype)
    padded[0:times, :] = data_ref[...]
    core = place_ref[0]
    every = padded[...]
    for which, out_ref in ((1 - core, send_ref), (core, keep_ref)):
        start = pl.multiple_of(which * half, half)
        out_ref[0:half, :] = dot_nt(maps_ref[pl.ds(start, half), :], every)
        upper = dot_nt(padded[pl.ds(start, half), :], every)
        lower = dot_nt(padded[pl.ds(block + start, half), :], padded[block:, :])
        row, col = grid_of(half, block)
        row = row + start
        diagonal = jnp.sum(jnp.where(row == col, lower, 0.0), axis=1, keepdims=True)
        out_ref[half:, 0:block] = jnp.where(col >= row, upper[:, 0:block], lower)
        out_ref[half:, block:] = jnp.where(col == times - block, diagonal, upper[:, block:])


def finish_kernel(times, people, chunk, pieces, place_ref, data_ref, *refs):
    own, other = refs[:pieces], refs[pieces : 2 * pieces]
    response_ref, maps_ref, total, packed, padded, sem = refs[2 * pieces :]
    load = pltpu.make_async_copy(data_ref, padded, sem)
    load.start()
    comps, full = total.shape
    half, block = comps // 2, full // 2
    core, spot, side = place_ref[0], place_ref[1], place_ref[2]
    for which, parts in ((core, own), (1 - core, other)):
        for d in range(pieces):
            at = pl.multiple_of(which * half + (spot ^ d) * chunk, 8)
            total[pl.ds(at, chunk), :] = parts[d][0:chunk, :]
        for d in range(2):
            at = pl.multiple_of(which * half + (side ^ d) * (half // 2), 8)
            packed[pl.ds(at, half // 2), :] = parts[d][chunk:, :]
    response = total[...] / people
    response_ref[...] = response.T[0:times, :]
    signal = response.astype(jnp.bfloat16)
    first, second = signal[:, 0:block], signal[:, block:]
    row, col = grid_of(comps, block)
    corner = packed[:, 0:block]
    beside = packed[:, block:]
    last = jnp.sum(jnp.where(col == times - block, beside, 0.0), axis=1, keepdims=True)
    u11 = jnp.where(col > row, corner, jnp.where(col == row, 0.5 * corner, 0.0))
    u22 = jnp.where(col < row, corner, jnp.where(col == row, 0.5 * last, 0.0))
    u12 = jnp.where(col < times - block, beside, 0.0)

    def dot2(a, b):
        high, low = split(b)
        return dot(a, high) + dot(a, low)

    left = dot2(first, u11)
    right = dot2(first, u12) + dot2(second, u22)
    lh, ll = split(left)
    rh, rl = split(right)
    product = (dot_nt(lh, first) + dot_nt(ll, first)) + (dot_nt(rh, second) + dot_nt(rl, second))
    gram = product + product.T
    scale = jnp.sqrt(jnp.sum(gram * gram) + 1e-06)
    row, col = grid_of(comps, comps)
    identity = jnp.where(row == col, 1.5, 0.0)
    estimate = gram / scale
    inverse = identity - 0.5 * estimate
    estimate = dot3(estimate, inverse)
    for step in range(1, NS_STEPS):
        middle = identity - 0.5 * dot3(inverse, estimate)
        if step < NS_STEPS - 1:
            estimate = dot3(estimate, middle)
        inverse = dot3(middle, inverse)
    factor = inverse / jnp.sqrt(scale)
    fh, fl = split(factor)
    weights = dot(fh, signal) + dot(fl, signal)
    wh, wl = split(weights[:, 0:times])
    load.wait()
    data = padded[...]
    maps_ref[...] = (dot(wh, data) + dot(wl, data)).astype(jnp.bfloat16)


def exchange(value, subjects, voxels, subj_step, vox_step):
    pairs = [
        (s * voxels + v, (s ^ subj_step) * voxels + (v ^ vox_step))
        for s in range(subjects)
        for v in range(voxels)
    ]
    return lax.ppermute(value, AXES, pairs)


def shards(data, maps):
    subjects, voxels = lax.axis_size("subj"), lax.axis_size("vox")
    _, times, wide = data.shape
    comps = maps.shape[1]
    people = subjects * data.shape[0]
    full, half = 2 * comps, comps // 2
    spots = 2 * subjects
    chunk = half // spots
    swap = functools.partial(exchange, subjects=subjects, voxels=voxels)
    s, v = lax.axis_index("subj"), lax.axis_index("vox")
    core, side = v % 2, v // 2 % 2
    spot = s * 2 + side
    place = jnp.stack([core, spot, side]).astype(jnp.int32)
    smem = pl.BlockSpec(memory_space=pltpu.SMEM)
    vmem = pl.BlockSpec(memory_space=pltpu.VMEM)
    params = pltpu.CompilerParams(vmem_limit_bytes=VMEM_LIMIT)

    send, keep = pl.pallas_call(
        functools.partial(partials_kernel, times),
        out_shape=[jax.ShapeDtypeStruct((comps, full), jnp.float32)] * 2,
        in_specs=[smem, vmem, vmem],
        out_specs=[vmem, vmem],
        scratch_shapes=[pltpu.VMEM((full, wide), jnp.bfloat16)],
        compiler_params=params,
        name="partials",
    )(place, data[0], maps[0])
    halves = keep + swap(send, subj_step=0, vox_step=1)

    def of_response(at):
        return lax.dynamic_slice_in_dim(halves, at * chunk, chunk, 0)

    def of_both(spot_at, side_at):
        square = lax.dynamic_slice_in_dim(halves, half + side_at * (half // 2), half // 2, 0)
        return jnp.concatenate([of_response(spot_at), square], 0)

    def step_of(d):
        return dict(subj_step=d >> 1, vox_step=2 * (d & 1))

    got = [swap(of_both(spot ^ 1, side ^ 1), **step_of(1))]
    got += [swap(of_response(spot ^ d), **step_of(d)) for d in range(2, spots)]
    sums = of_both(spot, side) + got[0]
    sums = jnp.concatenate([sums[:chunk] + sum(got[1:]), sums[chunk:]], 0)
    step = 4
    while step < voxels:
        sums = sums + swap(sums, subj_step=0, vox_step=step)
        step *= 2
    own = [sums, swap(sums, **step_of(1))]
    own += [swap(sums[:chunk], **step_of(d)) for d in range(2, spots)]
    other = [swap(piece, subj_step=0, vox_step=1) for piece in own]

    response, new_maps = pl.pallas_call(
        functools.partial(finish_kernel, times, people, chunk, spots),
        out_shape=[
            jax.ShapeDtypeStruct((times, comps), jnp.float32),
            jax.ShapeDtypeStruct((comps, wide), jnp.bfloat16),
        ],
        in_specs=[smem, pl.BlockSpec(memory_space=pl.ANY)] + [vmem] * (2 * spots),
        out_specs=[vmem, vmem],
        scratch_shapes=[
            pltpu.VMEM((comps, full), jnp.float32),
            pltpu.VMEM((comps, full), jnp.float32),
            pltpu.VMEM((times, wide), jnp.bfloat16),
            pltpu.SemaphoreType.DMA,
        ],
        compiler_params=params,
        name="finish",
    )(place, data[0], *own, *other)
    return response, new_maps[None]


def solution(mesh):
    in_specs = (P("subj", None, "vox"), P("subj", None, "vox"))
    out_specs = (P(), P("subj", None, "vox"))
    return jax.shard_map(shards, mesh=mesh, in_specs=in_specs, out_specs=out_specs, check_vma=False)
```

```python
import functools

import jax
import jax.numpy as jnp
from jax import lax
from jax.experimental import pallas as pl
from jax.experimental.pallas import tpu as pltpu
from jax.sharding import PartitionSpec as P

NS_STEPS = 5
VMEM_LIMIT = 40 * 1024 * 1024
AXES = ("subj", "vox")
NT = (((1,), (1,)), ((), ()))


def dot(a, b):
    return jnp.dot(a, b, preferred_element_type=jnp.float32)


def dot_nt(a, b):
    return lax.dot_general(a, b, NT, preferred_element_type=jnp.float32)


def split(a):
    high = a.astype(jnp.bfloat16)
    return high, (a - high.astype(jnp.float32)).astype(jnp.bfloat16)


def dot3(a, b):
    (ah, al), (bh, bl) = split(a), split(b)
    return dot(ah, bh) + (dot(ah, bl) + dot(al, bh))


def grid_of(rows, cols):
    return (
        lax.broadcasted_iota(jnp.int32, (rows, cols), 0),
        lax.broadcasted_iota(jnp.int32, (rows, cols), 1),
    )


def partials_kernel(times, place_ref, data_ref, maps_ref, send_ref, keep_ref, padded):
    full, comps = padded.shape[0], maps_ref.shape[0]
    half, block = comps // 2, full // 2
    tail = times // 16 * 16
    padded[tail:, :] = jnp.zeros((full - tail, padded.shape[1]), padded.dtype)
    padded[0:times, :] = data_ref[...]
    core = place_ref[0]
    every = padded[...]
    for which, out_ref in ((1 - core, send_ref), (core, keep_ref)):
        start = pl.multiple_of(which * half, half)
        out_ref[0:half, :] = dot_nt(maps_ref[pl.ds(start, half), :], every)
        upper = dot_nt(padded[pl.ds(start, half), :], every)
        lower = dot_nt(padded[pl.ds(block + start, half), :], padded[block:, :])
        row, col = grid_of(half, block)
        row = row + start
        diagonal = jnp.sum(jnp.where(row == col, lower, 0.0), axis=1, keepdims=True)
        out_ref[half:, 0:block] = jnp.where(col >= row, upper[:, 0:block], lower)
        out_ref[half:, block:] = jnp.where(col == times - block, diagonal, upper[:, block:])


def finish_kernel(times, people, chunk, pieces, place_ref, data_ref, *refs):
    own, other = refs[: pieces + 2], refs[pieces + 2 : 2 * pieces + 4]
    response_ref, maps_ref, total, packed, padded, sem = refs[2 * pieces + 4 :]
    load = pltpu.make_async_copy(data_ref, padded, sem)
    load.start()
    comps, full = total.shape
    half, block = comps // 2, full // 2
    quarter, eighth = half // 2, half // 4
    core, spot, side, level = place_ref[0], place_ref[1], place_ref[2], place_ref[3]
    for which, parts in ((core, own), (1 - core, other)):
        for d in range(pieces):
            at = pl.multiple_of(which * half + (spot ^ d) * chunk, 8)
            total[pl.ds(at, chunk), :] = parts[2 + d][...]
        for d in range(4):
            at = which * half + (side ^ (d >> 1)) * quarter + (level ^ (d & 1)) * eighth
            piece = parts[d >> 1][(d & 1) * eighth : (d & 1) * eighth + eighth, :]
            packed[pl.ds(pl.multiple_of(at, 8), eighth), :] = piece
    response = total[...] / people
    response_ref[...] = response.T[0:times, :]
    signal = response.astype(jnp.bfloat16)
    first, second = signal[:, 0:block], signal[:, block:]
    row, col = grid_of(comps, block)
    corner = packed[:, 0:block]
    beside = packed[:, block:]
    last = jnp.sum(jnp.where(col == times - block, beside, 0.0), axis=1, keepdims=True)
    u11 = jnp.where(col > row, corner, jnp.where(col == row, 0.5 * corner, 0.0))
    u22 = jnp.where(col < row, corner, jnp.where(col == row, 0.5 * last, 0.0))
    u12 = jnp.where(col < times - block, beside, 0.0)

    def dot2(a, b):
        high, low = split(b)
        return dot(a, high) + dot(a, low)

    left = dot2(first, u11)
    right = dot2(first, u12) + dot2(second, u22)
    lh, ll = split(left)
    rh, rl = split(right)
    product = (dot_nt(lh, first) + dot_nt(ll, first)) + (dot_nt(rh, second) + dot_nt(rl, second))
    gram = product + product.T
    scale = jnp.sqrt(jnp.sum(gram * gram) + 1e-06)
    row, col = grid_of(comps, comps)
    identity = jnp.where(row == col, 1.5, 0.0)
    estimate = gram / scale
    inverse = identity - 0.5 * estimate
    estimate = dot3(estimate, inverse)
    for step in range(1, NS_STEPS):
        middle = identity - 0.5 * dot3(inverse, estimate)
        if step < NS_STEPS - 1:
            estimate = dot3(estimate, middle)
        inverse = dot3(middle, inverse)
    factor = inverse / jnp.sqrt(scale)
    fh, fl = split(factor)
    weights = dot(fh, signal) + dot(fl, signal)
    wh, wl = split(weights[:, 0:times])
    load.wait()
    data = padded[...]
    maps_ref[...] = (dot(wh, data) + dot(wl, data)).astype(jnp.bfloat16)


def exchange(value, subjects, voxels, subj_step, vox_step):
    pairs = [
        (s * voxels + v, (s ^ subj_step) * voxels + (v ^ vox_step))
        for s in range(subjects)
        for v in range(voxels)
    ]
    return lax.ppermute(value, AXES, pairs)


def shards(data, maps):
    subjects, voxels = lax.axis_size("subj"), lax.axis_size("vox")
    _, times, wide = data.shape
    comps = maps.shape[1]
    people = subjects * data.shape[0]
    full, half = 2 * comps, comps // 2
    spots = 2 * subjects
    chunk = half // spots
    swap = functools.partial(exchange, subjects=subjects, voxels=voxels)
    s, v = lax.axis_index("subj"), lax.axis_index("vox")
    core, side = v % 2, v // 2 % 2
    spot, level = s * 2 + side, v // 4 % 2
    place = jnp.stack([core, spot, side, level]).astype(jnp.int32)
    smem = pl.BlockSpec(memory_space=pltpu.SMEM)
    vmem = pl.BlockSpec(memory_space=pltpu.VMEM)
    params = pltpu.CompilerParams(vmem_limit_bytes=VMEM_LIMIT)

    send, keep = pl.pallas_call(
        functools.partial(partials_kernel, times),
        out_shape=[jax.ShapeDtypeStruct((comps, full), jnp.float32)] * 2,
        in_specs=[smem, vmem, vmem],
        out_specs=[vmem, vmem],
        scratch_shapes=[pltpu.VMEM((full, wide), jnp.bfloat16)],
        compiler_params=params,
        name="partials",
    )(place, data[0], maps[0])
    halves = keep + swap(send, subj_step=0, vox_step=1)

    def rows(value, at, size):
        return lax.dynamic_slice_in_dim(value, at * size, size, 0)

    def spot_step(d):
        return dict(subj_step=d >> 1, vox_step=2 * (d & 1))

    sums, square = halves[:half], halves[half:]
    got = [swap(rows(sums, spot ^ d, chunk), **spot_step(d)) for d in range(1, spots)]
    sums = rows(sums, spot, chunk) + sum(got)
    quarter, eighth = half // 2, half // 4
    square = rows(square, side, quarter) + swap(rows(square, side ^ 1, quarter), subj_step=0, vox_step=2)
    square = rows(square, level, eighth) + swap(rows(square, level ^ 1, eighth), subj_step=0, vox_step=4)
    sums = sums + swap(sums, subj_step=0, vox_step=4)
    step = 8
    while step < voxels:
        square = square + swap(square, subj_step=0, vox_step=step)
        sums = sums + swap(sums, subj_step=0, vox_step=step)
        step *= 2
    square = jnp.concatenate([square, swap(square, subj_step=0, vox_step=4)], 0)
    own = [square, swap(square, subj_step=0, vox_step=2), sums]
    own += [swap(sums, **spot_step(d)) for d in range(1, spots)]
    other = [swap(piece, subj_step=0, vox_step=1) for piece in own]

    response, new_maps = pl.pallas_call(
        functools.partial(finish_kernel, times, people, chunk, spots),
        out_shape=[
            jax.ShapeDtypeStruct((times, comps), jnp.float32),
            jax.ShapeDtypeStruct((comps, wide), jnp.bfloat16),
        ],
        in_specs=[smem, pl.BlockSpec(memory_space=pl.ANY)] + [vmem] * (2 * spots + 4),
        out_specs=[vmem, vmem],
        scratch_shapes=[
            pltpu.VMEM((comps, full), jnp.float32),
            pltpu.VMEM((comps, full), jnp.float32),
            pltpu.VMEM((times, wide), jnp.bfloat16),
            pltpu.SemaphoreType.DMA,
        ],
        compiler_params=params,
        name="finish",
    )(place, data[0], *own, *other)
    return response, new_maps[None]


def solution(mesh):
    in_specs = (P("subj", None, "vox"), P("subj", None, "vox"))
    out_specs = (P(), P("subj", None, "vox"))
    return jax.shard_map(shards, mesh=mesh, in_specs=in_specs, out_specs=out_specs, check_vma=False)
```

```python
import functools

import jax
import jax.numpy as jnp
from jax import lax
from jax.experimental import pallas as pl
from jax.experimental.pallas import tpu as pltpu
from jax.sharding import PartitionSpec as P

NS_STEPS = 5
VMEM_LIMIT = 40 * 1024 * 1024
AXES = ("subj", "vox")
NT = (((1,), (1,)), ((), ()))


def dot(a, b):
    return jnp.dot(a, b, preferred_element_type=jnp.float32)


def dot_nt(a, b):
    return lax.dot_general(a, b, NT, preferred_element_type=jnp.float32)


def split(a):
    high = a.astype(jnp.bfloat16)
    return high, (a - high.astype(jnp.float32)).astype(jnp.bfloat16)


def dot3(a, b):
    (ah, al), (bh, bl) = split(a), split(b)
    return dot(ah, bh) + (dot(ah, bl) + dot(al, bh))


def grid_of(rows, cols):
    return (
        lax.broadcasted_iota(jnp.int32, (rows, cols), 0),
        lax.broadcasted_iota(jnp.int32, (rows, cols), 1),
    )


def partials_kernel(times, data_ref, maps_ref, sums_ref, square_ref, raw, weights, padded, cross, sems):
    parts = raw.shape[0]
    part = raw.shape[2]
    loads = []
    for k in range(parts):
        at = pl.ds(k * part, part)
        loads.append(pltpu.make_async_copy(data_ref.at[:, at], raw.at[k], sems.at[0, k]))
        loads.append(pltpu.make_async_copy(maps_ref.at[:, at], weights.at[k], sems.at[1, k]))
    for load in loads:
        load.start()
    full, comps = padded.shape[0], weights.shape[1]
    tail = times // 16 * 16
    padded[tail:, :] = jnp.zeros((full - tail, part), padded.dtype)
    for k in range(parts):
        loads[2 * k].wait()
        loads[2 * k + 1].wait()
        padded[0:times, :] = raw[k]
        every = padded[...]
        upper, lower = every[0:comps], every[comps:]
        terms = dot_nt(weights[k], every), dot_nt(upper, every), dot_nt(lower, lower)
        for ref, term in zip((sums_ref, square_ref, cross), terms):
            ref[...] = term if k == 0 else ref[...] + term
    row, col = grid_of(comps, comps)
    lower = cross[...]
    diagonal = jnp.sum(jnp.where(row == col, lower, 0.0), axis=1, keepdims=True)
    square_ref[:, 0:comps] = jnp.where(col >= row, square_ref[:, 0:comps], lower)
    square_ref[:, comps:] = jnp.where(col == times - comps, diagonal, square_ref[:, comps:])


def finish_kernel(times, people, chunk, pieces, place_ref, data_ref, *refs):
    own, other = refs[: pieces + 2], refs[pieces + 2 : 2 * pieces + 4]
    response_ref, maps_ref, total, packed, raw, turned, new, sems = refs[2 * pieces + 4 :]
    load = pltpu.make_async_copy(data_ref, raw, sems.at[0])
    load.start()
    comps, full = total.shape
    half, block = comps // 2, full // 2
    quarter, eighth = half // 2, half // 4
    core, spot, side, level = place_ref[0], place_ref[1], place_ref[2], place_ref[3]
    for which, parts in ((core, own), (1 - core, other)):
        for d in range(pieces):
            at = pl.multiple_of(which * half + (spot ^ d) * chunk, 8)
            total[pl.ds(at, chunk), :] = parts[2 + d][...]
        for d in range(4):
            at = which * half + (side ^ (d >> 1)) * quarter + (level ^ (d & 1)) * eighth
            piece = parts[d >> 1][(d & 1) * eighth : (d & 1) * eighth + eighth, :]
            packed[pl.ds(pl.multiple_of(at, 8), eighth), :] = piece
    response = total[...] / people
    turned[...] = response.T[0:times, :]
    answer = pltpu.make_async_copy(turned, response_ref, sems.at[1])
    answer.start()
    signal = response.astype(jnp.bfloat16)
    first, second = signal[:, 0:block], signal[:, block:]
    row, col = grid_of(comps, block)
    corner = packed[:, 0:block]
    beside = packed[:, block:]
    last = jnp.sum(jnp.where(col == times - block, beside, 0.0), axis=1, keepdims=True)
    u11 = jnp.where(col > row, corner, jnp.where(col == row, 0.5 * corner, 0.0))
    u22 = jnp.where(col < row, corner, jnp.where(col == row, 0.5 * last, 0.0))
    u12 = jnp.where(col < times - block, beside, 0.0)

    def dot2(a, b):
        high, low = split(b)
        return dot(a, high) + dot(a, low)

    left = dot2(first, u11)
    right = dot2(first, u12) + dot2(second, u22)
    lh, ll = split(left)
    rh, rl = split(right)
    product = (dot_nt(lh, first) + dot_nt(ll, first)) + (dot_nt(rh, second) + dot_nt(rl, second))
    gram = product + product.T
    scale = jnp.sqrt(jnp.sum(gram * gram) + 1e-06)
    row, col = grid_of(comps, comps)
    identity = jnp.where(row == col, 1.5, 0.0)
    estimate = gram / scale
    inverse = identity - 0.5 * estimate
    estimate = dot3(estimate, inverse)
    for step in range(1, NS_STEPS):
        middle = identity - 0.5 * dot3(inverse, estimate)
        if step < NS_STEPS - 1:
            estimate = dot3(estimate, middle)
        inverse = dot3(middle, inverse)
    factor = inverse / jnp.sqrt(scale)
    fh, fl = split(factor)
    weights = dot(fh, signal) + dot(fl, signal)
    both = jnp.concatenate(split(weights[:, 0:times]), 0)
    load.wait()
    stores = []
    part = new.shape[2]
    for k in range(new.shape[0]):
        at = pl.ds(k * part, part)
        result = dot(both, raw[:, at])
        new[k] = (result[0:comps] + result[comps:]).astype(jnp.bfloat16)
        stores.append(pltpu.make_async_copy(new.at[k], maps_ref.at[:, at], sems.at[2 + k]))
        stores[-1].start()
    for store in [answer, *stores]:
        store.wait()


def exchange(value, subjects, voxels, subj_step, vox_step):
    pairs = [
        (s * voxels + v, (s ^ subj_step) * voxels + (v ^ vox_step))
        for s in range(subjects)
        for v in range(voxels)
    ]
    return lax.ppermute(value, AXES, pairs)


def shards(data, maps):
    subjects, voxels = lax.axis_size("subj"), lax.axis_size("vox")
    _, times, wide = data.shape
    comps = maps.shape[1]
    people = subjects * data.shape[0]
    full, half = 2 * comps, comps // 2
    spots = 2 * subjects
    chunk = half // spots
    swap = functools.partial(exchange, subjects=subjects, voxels=voxels)
    s, v = lax.axis_index("subj"), lax.axis_index("vox")
    core, side = v & 1, (v >> 1) & 1
    spot, level = s * 2 + side, (v >> 2) & 1
    place = jnp.stack([core, spot, side, level]).astype(jnp.int32)
    smem = pl.BlockSpec(memory_space=pltpu.SMEM)
    vmem = pl.BlockSpec(memory_space=pltpu.VMEM)
    params = pltpu.CompilerParams(vmem_limit_bytes=VMEM_LIMIT)

    whole = pl.BlockSpec(memory_space=pltpu.HBM)
    parts = 2 if wide % 512 == 0 else 1
    sums, square = pl.pallas_call(
        functools.partial(partials_kernel, times),
        out_shape=[jax.ShapeDtypeStruct((comps, full), jnp.float32)] * 2,
        in_specs=[whole, whole],
        out_specs=[vmem, vmem],
        scratch_shapes=[
            pltpu.VMEM((parts, times, wide // parts), jnp.bfloat16),
            pltpu.VMEM((parts, comps, wide // parts), jnp.bfloat16),
            pltpu.VMEM((full, wide // parts), jnp.bfloat16),
            pltpu.VMEM((comps, comps), jnp.float32),
            pltpu.SemaphoreType.DMA((2, parts)),
        ],
        compiler_params=params,
        name="partials",
    )(*(pltpu.with_memory_space_constraint(value[0], pltpu.HBM) for value in (data, maps)))

    def rows(value, at, size):
        return lax.dynamic_slice_in_dim(value, at * size, size, 0)

    def spot_step(d):
        return dict(subj_step=d >> 1, vox_step=2 * (d & 1))

    square = rows(square, core, half) + swap(rows(square, 1 - core, half), subj_step=0, vox_step=1)
    sums = rows(sums, core, half) + swap(rows(sums, 1 - core, half), subj_step=0, vox_step=1)
    quarter, eighth = half // 2, half // 4
    square = rows(square, side, quarter) + swap(rows(square, side ^ 1, quarter), subj_step=0, vox_step=2)
    got = [swap(rows(sums, spot ^ d, chunk), **spot_step(d)) for d in range(1, spots)]
    sums = rows(sums, spot, chunk) + sum(got)
    square = rows(square, level, eighth) + swap(rows(square, level ^ 1, eighth), subj_step=0, vox_step=4)
    sums = sums + swap(sums, subj_step=0, vox_step=4)
    step = 8
    while step < voxels:
        square = square + swap(square, subj_step=0, vox_step=step)
        sums = sums + swap(sums, subj_step=0, vox_step=step)
        step *= 2
    square = jnp.concatenate([square, swap(square, subj_step=0, vox_step=4)], 0)
    square, sums = lax.optimization_barrier((square, sums))
    own = [square, swap(square, subj_step=0, vox_step=2), sums]
    own += [swap(sums, **spot_step(d)) for d in range(1, spots)]
    other = [swap(piece, subj_step=0, vox_step=1) for piece in own]

    response, new_maps = pl.pallas_call(
        functools.partial(finish_kernel, times, people, chunk, spots),
        out_shape=[
            jax.ShapeDtypeStruct((times, comps), jnp.float32),
            jax.ShapeDtypeStruct((comps, wide), jnp.bfloat16),
        ],
        in_specs=[smem, whole] + [vmem] * (2 * spots + 4),
        out_specs=[whole, whole],
        scratch_shapes=[
            pltpu.VMEM((comps, full), jnp.float32),
            pltpu.VMEM((comps, full), jnp.float32),
            pltpu.VMEM((times, wide), jnp.bfloat16),
            pltpu.VMEM((times, comps), jnp.float32),
            pltpu.VMEM((parts, comps, wide // parts), jnp.bfloat16),
            pltpu.SemaphoreType.DMA((2 + parts,)),
        ],
        compiler_params=params,
        name="finish",
    )(place, data[0], *own, *other)
    return response, new_maps[None]


def solution(mesh):
    in_specs = (P("subj", None, "vox"), P("subj", None, "vox"))
    out_specs = (P(), P("subj", None, "vox"))
    return jax.shard_map(shards, mesh=mesh, in_specs=in_specs, out_specs=out_specs, check_vma=False)
```

```python
import functools

import jax
import jax.numpy as jnp
from jax import lax
from jax.experimental import pallas as pl
from jax.experimental.pallas import tpu as pltpu
from jax.sharding import PartitionSpec as P

TILE = 128
VMEM_LIMIT = 40 * 1024 * 1024
AXES = ("subj", "vox")
NT = (((1,), (1,)), ((), ()))


def dot(a, b):
    return jnp.dot(a, b, preferred_element_type=jnp.float32)


def dot_nt(a, b):
    return lax.dot_general(a, b, NT, preferred_element_type=jnp.float32)


def split(a):
    high = a.astype(jnp.bfloat16)
    return high, (a - high.astype(jnp.float32)).astype(jnp.bfloat16)


def dot3(a, b):
    (ah, al), (bh, bl) = split(a), split(b)
    return dot(ah, bh) + (dot(ah, bl) + dot(al, bh))


def grid_of(rows, cols):
    return (
        lax.broadcasted_iota(jnp.int32, (rows, cols), 0),
        lax.broadcasted_iota(jnp.int32, (rows, cols), 1),
    )


def response_kernel(times, data_ref, maps_ref, sums_ref, padded_ref, raw, weights, sems):
    parts, comps, part = weights.shape
    loads = []
    for k in range(parts):
        at = pl.ds(k * part, part)
        loads.append(pltpu.make_async_copy(data_ref.at[:, at], raw.at[k], sems.at[0, k]))
        loads.append(pltpu.make_async_copy(maps_ref.at[:, at], weights.at[k], sems.at[1, k]))
    for load in loads:
        load.start()
    full, wide = padded_ref.shape
    tail = times // 16 * 16
    padded_ref[tail:, :] = jnp.zeros((full - tail, wide), padded_ref.dtype)
    for k in range(parts):
        at = pl.ds(k * part, part)
        loads[2 * k].wait()
        loads[2 * k + 1].wait()
        padded_ref[0:times, at] = raw[k]
        term = dot_nt(weights[k], padded_ref[:, at])
        sums_ref[...] = term if k == 0 else sums_ref[...] + term


def square_kernel(times, padded_ref, square_ref):
    comps = square_ref.shape[0]
    upper = dot_nt(padded_ref[0:comps, :], padded_ref[...])
    lower = dot_nt(padded_ref[comps:, :], padded_ref[comps:, :])
    row, col = grid_of(comps, comps)
    diagonal = jnp.sum(jnp.where(row == col, lower, 0.0), axis=1, keepdims=True)
    square_ref[:, 0:comps] = jnp.where(col >= row, upper[:, 0:comps], lower)
    square_ref[:, comps:] = jnp.where(col == times - comps, diagonal, upper[:, comps:])


def finish_kernel(times, people, chunk, place_ref, data_ref, *refs):
    pieces, (response_ref, maps_ref, total, packed, turned, new, sems) = refs[:8], refs[8:]
    comps, full = total.shape
    half, block = comps // 2, full // 2
    quarter, eighth = half // 2, half // 4
    core, spot, side, level = place_ref[0], place_ref[1], place_ref[2], place_ref[3]
    for which, parts in ((core, pieces[0:4]), (1 - core, pieces[4:8])):
        for d in range(half // chunk):
            at = which * half + (spot ^ d) * chunk
            piece = parts[d * chunk // quarter][d * chunk % quarter : d * chunk % quarter + chunk, :]
            total[pl.ds(pl.multiple_of(at, 8), chunk), :] = piece
        for d in range(4):
            at = which * half + (side ^ (d >> 1)) * quarter + (level ^ (d & 1)) * eighth
            piece = parts[2 + (d >> 1)][(d & 1) * eighth : (d & 1) * eighth + eighth, :]
            packed[pl.ds(pl.multiple_of(at, 8), eighth), :] = piece
    response = total[...] / people

    def turn(k):
        size = min(times - k * TILE, TILE)
        turned[k * TILE : k * TILE + size, :] = response[:, k * TILE : (k + 1) * TILE].T[0:size, :]

    signal = response.astype(jnp.bfloat16)
    first, second = signal[:, 0:block], signal[:, block:]
    row, col = grid_of(comps, block)
    corner = packed[:, 0:block]
    beside = packed[:, block:]
    last = jnp.sum(jnp.where(col == times - block, beside, 0.0), axis=1, keepdims=True)
    u11 = jnp.where(col > row, corner, jnp.where(col == row, 0.5 * corner, 0.0))
    u22 = jnp.where(col < row, corner, jnp.where(col == row, 0.5 * last, 0.0))
    u12 = jnp.where(col < times - block, beside, 0.0)

    def dot2(a, b):
        high, low = split(b)
        return dot(a, high) + dot(a, low)

    left = dot2(first, u11)
    right = dot2(first, u12) + dot2(second, u22)
    lh, ll = split(left)
    rh, rl = split(right)
    product = (dot_nt(lh, first) + dot_nt(ll, first)) + (dot_nt(rh, second) + dot_nt(rl, second))
    gram = product + product.T
    squared = jnp.sum(gram * gram) + 1e-06
    scale = jnp.sqrt(squared)
    row, col = grid_of(comps, comps)
    diagonal = jnp.where(row == col, 1.0, 0.0)

    def two_steps(t, t2):
        inner = 1.6875 * diagonal - 0.5625 * t + 0.0625 * t2
        return 2.25 * diagonal - 2.4375 * t + dot3(t2, inner)

    t2 = dot3(gram, gram) / squared
    t = gram / scale
    turn(0)
    inverse = two_steps(t, t2)
    turn(1)
    t = dot3(dot3(t, inverse), inverse)
    turn(2)
    step = two_steps(t, dot3(t, t))
    turn(3)
    t = dot3(dot3(t, step), step)
    inverse = dot3(inverse, step)
    answer = pltpu.make_async_copy(turned, response_ref, sems.at[0])
    answer.start()
    inverse = 1.5 * inverse - 0.5 * dot3(inverse, t)
    factor = inverse / jnp.sqrt(scale)
    fh, fl = split(factor)
    weights = dot(fh, signal) + dot(fl, signal)
    both = jnp.concatenate(split(weights), 0)
    stores = []
    part = new.shape[2]
    for k in range(new.shape[0]):
        at = pl.ds(k * part, part)
        result = dot(both, data_ref[:, at])
        new[k] = (result[0:comps] + result[comps:]).astype(jnp.bfloat16)
        stores.append(pltpu.make_async_copy(new.at[k], maps_ref.at[:, at], sems.at[1 + k]))
        stores[-1].start()
    for store in [answer, *stores]:
        store.wait()


def exchange(value, subjects, voxels, subj_step, vox_step):
    pairs = [
        (s * voxels + v, (s ^ subj_step) * voxels + (v ^ vox_step))
        for s in range(subjects)
        for v in range(voxels)
    ]
    return lax.ppermute(value, AXES, pairs)


def shards(data, maps):
    subjects, voxels = lax.axis_size("subj"), lax.axis_size("vox")
    _, times, wide = data.shape
    comps = maps.shape[1]
    people = subjects * data.shape[0]
    full, half = 2 * comps, comps // 2
    spots = 2 * subjects
    chunk = half // spots
    swap = functools.partial(exchange, subjects=subjects, voxels=voxels)
    s, v = lax.axis_index("subj"), lax.axis_index("vox")
    core, side = v & 1, (v >> 1) & 1
    spot, level = s * 2 + side, (v >> 2) & 1
    place = jnp.stack([core, spot, side, level]).astype(jnp.int32)
    smem = pl.BlockSpec(memory_space=pltpu.SMEM)
    vmem = pl.BlockSpec(memory_space=pltpu.VMEM)
    params = pltpu.CompilerParams(vmem_limit_bytes=VMEM_LIMIT)

    whole = pl.BlockSpec(memory_space=pltpu.HBM)
    parts = 2 if wide % 512 == 0 else 1
    sums, padded = pl.pallas_call(
        functools.partial(response_kernel, times),
        out_shape=[
            jax.ShapeDtypeStruct((comps, full), jnp.float32),
            jax.ShapeDtypeStruct((full, wide), jnp.bfloat16),
        ],
        in_specs=[whole, whole],
        out_specs=[vmem, vmem],
        scratch_shapes=[
            pltpu.VMEM((parts, times, wide // parts), jnp.bfloat16),
            pltpu.VMEM((parts, comps, wide // parts), jnp.bfloat16),
            pltpu.SemaphoreType.DMA((2, parts)),
        ],
        compiler_params=params,
        name="response_terms",
    )(*(pltpu.with_memory_space_constraint(value[0], pltpu.HBM) for value in (data, maps)))
    square = pl.pallas_call(
        functools.partial(square_kernel, times),
        out_shape=jax.ShapeDtypeStruct((comps, full), jnp.float32),
        in_specs=[vmem],
        out_specs=vmem,
        compiler_params=params,
        cost_estimate=pl.CostEstimate(flops=6 * comps * comps * wide, bytes_accessed=full * wide * 2, transcendentals=0),
        name="square_terms",
    )(padded)

    def rows(value, at, size):
        return lax.dynamic_slice_in_dim(value, at * size, size, 0)

    def over_core(value):
        return swap(value, subj_step=0, vox_step=1)

    def over_side(value):
        return swap(value, subj_step=0, vox_step=2)

    quarter, eighth = half // 2, half // 4
    sums = rows(sums, core, half) + over_core(rows(sums, 1 - core, half))
    square = rows(square, core, half) + over_core(rows(square, 1 - core, half))

    bits = [1 << k for k in range(subjects.bit_length() - 1)]
    for bit in reversed(bits):
        size = sums.shape[0] // 2
        mine = jnp.where(s & bit > 0, 1, 0)
        sums = rows(sums, mine, size) + swap(rows(sums, 1 - mine, size), subj_step=bit, vox_step=0)
    sums = rows(sums, side, chunk) + over_side(rows(sums, 1 - side, chunk))
    step = 4
    while step < voxels:
        sums = sums + swap(sums, subj_step=0, vox_step=step)
        step *= 2
    sums = jnp.concatenate([sums, over_side(sums)], 0)
    for bit in bits[:-1]:
        sums = jnp.concatenate([sums, swap(sums, subj_step=bit, vox_step=0)], 0)
    responses = [sums, swap(sums, subj_step=bits[-1], vox_step=0)]

    square = rows(square, side, quarter) + over_side(rows(square, 1 - side, quarter))
    square = rows(square, level, eighth) + swap(rows(square, 1 - level, eighth), subj_step=0, vox_step=4)
    step = 8
    while step < voxels:
        square = square + swap(square, subj_step=0, vox_step=step)
        step *= 2
    square = jnp.concatenate([square, swap(square, subj_step=0, vox_step=4)], 0)
    squares = [square, over_side(square)]
    pieces = responses + squares
    pieces += [over_core(piece) for piece in pieces]

    response, new_maps = pl.pallas_call(
        functools.partial(finish_kernel, times, people, chunk),
        out_shape=[
            jax.ShapeDtypeStruct((times, comps), jnp.float32),
            jax.ShapeDtypeStruct((comps, wide), jnp.bfloat16),
        ],
        in_specs=[smem, vmem] + [vmem] * len(pieces),
        out_specs=[whole, whole],
        scratch_shapes=[
            pltpu.VMEM((comps, full), jnp.float32),
            pltpu.VMEM((comps, full), jnp.float32),
            pltpu.VMEM((times, comps), jnp.float32),
            pltpu.VMEM((parts, comps, wide // parts), jnp.bfloat16),
            pltpu.SemaphoreType.DMA((1 + parts,)),
        ],
        compiler_params=params,
        name="finish",
    )(place, padded, *pieces)
    return response, new_maps[None]


def solution(mesh):
    in_specs = (P("subj", None, "vox"), P("subj", None, "vox"))
    out_specs = (P(), P("subj", None, "vox"))
    return jax.shard_map(shards, mesh=mesh, in_specs=in_specs, out_specs=out_specs, check_vma=False)
```

```python
import functools

import jax
import jax.numpy as jnp
from jax import lax
from jax.experimental import pallas as pl
from jax.experimental.pallas import tpu as pltpu
from jax.sharding import PartitionSpec as P

TILE = 128
VMEM_LIMIT = 40 * 1024 * 1024
AXES = ("subj", "vox")
NT = (((1,), (1,)), ((), ()))


def dot(a, b):
    return jnp.dot(a, b, preferred_element_type=jnp.float32)


def dot_nt(a, b):
    return lax.dot_general(a, b, NT, preferred_element_type=jnp.float32)


def split(a):
    high = a.astype(jnp.bfloat16)
    return high, (a - high.astype(jnp.float32)).astype(jnp.bfloat16)


def dot3(a, b):
    (ah, al), (bh, bl) = split(a), split(b)
    rows = a.shape[0]
    product = dot(jnp.concatenate([ah, al], 0), bh)
    return product[:rows] + (product[rows:] + dot(ah, bl))


def grid_of(rows, cols):
    return (
        lax.broadcasted_iota(jnp.int32, (rows, cols), 0),
        lax.broadcasted_iota(jnp.int32, (rows, cols), 1),
    )


def response_kernel(times, data_ref, maps_ref, sums_ref, padded_ref, raw, weights, sems):
    parts, comps, part = weights.shape
    loads = []
    for k in range(parts):
        at = pl.ds(k * part, part)
        loads.append(pltpu.make_async_copy(data_ref.at[:, at], raw.at[k], sems.at[0, k]))
        loads.append(pltpu.make_async_copy(maps_ref.at[:, at], weights.at[k], sems.at[1, k]))
    for load in loads:
        load.start()
    full, wide = padded_ref.shape
    tail = times // 16 * 16
    padded_ref[tail:, :] = jnp.zeros((full - tail, wide), padded_ref.dtype)
    for k in range(parts):
        at = pl.ds(k * part, part)
        loads[2 * k].wait()
        loads[2 * k + 1].wait()
        padded_ref[0:times, at] = raw[k]
        term = dot_nt(weights[k], padded_ref[:, at])
        sums_ref[...] = term if k == 0 else sums_ref[...] + term


def square_kernel(times, padded_ref, square_ref):
    comps = square_ref.shape[0]
    upper = dot_nt(padded_ref[0:comps, :], padded_ref[...])
    lower = dot_nt(padded_ref[comps:, :], padded_ref[comps:, :])
    row, col = grid_of(comps, comps)
    diagonal = jnp.sum(jnp.where(row == col, lower, 0.0), axis=1, keepdims=True)
    square_ref[:, 0:comps] = jnp.where(col >= row, upper[:, 0:comps], lower)
    square_ref[:, comps:] = jnp.where(col == times - comps, diagonal, upper[:, comps:])


def finish_kernel(times, people, chunk, place_ref, data_ref, *refs):
    pieces, (response_ref, maps_ref, total, packed, turned, new, sems) = refs[:8], refs[8:]
    comps, full = total.shape
    half, block = comps // 2, full // 2
    quarter, eighth = half // 2, half // 4
    core, spot, side, level = place_ref[0], place_ref[1], place_ref[2], place_ref[3]
    for which, parts in ((core, pieces[0:4]), (1 - core, pieces[4:8])):
        for d in range(half // chunk):
            at = which * half + (spot ^ d) * chunk
            piece = parts[d * chunk // quarter][d * chunk % quarter : d * chunk % quarter + chunk, :]
            total[pl.ds(pl.multiple_of(at, 8), chunk), :] = piece
        for d in range(4):
            at = which * half + (side ^ (d >> 1)) * quarter + (level ^ (d & 1)) * eighth
            piece = parts[2 + (d >> 1)][(d & 1) * eighth : (d & 1) * eighth + eighth, :]
            packed[pl.ds(pl.multiple_of(at, 8), eighth), :] = piece
    response = total[...] / people

    def turn(k):
        size = min(times - k * TILE, TILE)
        turned[k * TILE : k * TILE + size, :] = response[:, k * TILE : (k + 1) * TILE].T[0:size, :]

    signal = response.astype(jnp.bfloat16)
    first, second = signal[:, 0:block], signal[:, block:]
    row, col = grid_of(comps, block)
    corner = packed[:, 0:block]
    beside = packed[:, block:]
    last = jnp.sum(jnp.where(col == times - block, beside, 0.0), axis=1, keepdims=True)
    u11 = jnp.where(col > row, corner, jnp.where(col == row, 0.5 * corner, 0.0))
    u22 = jnp.where(col < row, corner, jnp.where(col == row, 0.5 * last, 0.0))
    u12 = jnp.where(col < times - block, beside, 0.0)

    def dot2(a, b):
        high, low = split(b)
        return dot(a, high) + dot(a, low)

    left = dot2(first, u11)
    right = dot2(first, u12) + dot2(second, u22)
    lh, ll = split(left)
    rh, rl = split(right)
    product = (dot_nt(lh, first) + dot_nt(ll, first)) + (dot_nt(rh, second) + dot_nt(rl, second))
    gram = product + product.T
    scale = jnp.sqrt(jnp.sum(gram * gram) + 1e-06)
    row, col = grid_of(comps, comps)
    diagonal = jnp.where(row == col, 1.0, 0.0)

    def two_steps(t, t2):
        inner = 1.6875 * diagonal - 0.5625 * t + 0.0625 * t2
        return 2.25 * diagonal - 2.4375 * t + dot3(t2, inner)

    t = gram / scale
    t2 = dot3(t, t)
    turn(0)
    first_two = two_steps(t, t2)
    turn(1)
    t = dot3(dot3(t, first_two), first_two)
    turn(2)
    t2 = dot3(t, t)
    moved = dot3(first_two, t)
    next_two = two_steps(t, t2)
    turn(3)
    inverse = dot3(first_two, next_two)
    moved = dot3(moved, next_two)
    cubed = dot3(next_two, next_two)
    answer = pltpu.make_async_copy(turned, response_ref, sems.at[0])
    answer.start()
    inverse = 1.5 * inverse - 0.5 * dot3(moved, cubed)
    factor = inverse / jnp.sqrt(scale)
    fh, fl = split(factor)
    weights = dot(fh, signal) + dot(fl, signal)
    both = jnp.concatenate(split(weights), 0)
    stores = []
    part = new.shape[2]
    for k in range(new.shape[0]):
        at = pl.ds(k * part, part)
        result = dot(both, data_ref[:, at])
        new[k] = (result[0:comps] + result[comps:]).astype(jnp.bfloat16)
        stores.append(pltpu.make_async_copy(new.at[k], maps_ref.at[:, at], sems.at[1 + k]))
        stores[-1].start()
    for store in [answer, *stores]:
        store.wait()


def exchange(value, subjects, voxels, subj_step, vox_step):
    pairs = [
        (s * voxels + v, (s ^ subj_step) * voxels + (v ^ vox_step))
        for s in range(subjects)
        for v in range(voxels)
    ]
    return lax.ppermute(value, AXES, pairs)


def shards(data, maps):
    subjects, voxels = lax.axis_size("subj"), lax.axis_size("vox")
    _, times, wide = data.shape
    comps = maps.shape[1]
    people = subjects * data.shape[0]
    full, half = 2 * comps, comps // 2
    spots = 2 * subjects
    chunk = half // spots
    swap = functools.partial(exchange, subjects=subjects, voxels=voxels)
    s, v = lax.axis_index("subj"), lax.axis_index("vox")
    core, side = v & 1, (v >> 1) & 1
    spot, level = s * 2 + side, (v >> 2) & 1
    place = jnp.stack([core, spot, side, level]).astype(jnp.int32)
    smem = pl.BlockSpec(memory_space=pltpu.SMEM)
    vmem = pl.BlockSpec(memory_space=pltpu.VMEM)
    params = pltpu.CompilerParams(vmem_limit_bytes=VMEM_LIMIT)

    whole = pl.BlockSpec(memory_space=pltpu.HBM)
    parts = 2 if wide % 512 == 0 else 1
    sums, padded = pl.pallas_call(
        functools.partial(response_kernel, times),
        out_shape=[
            jax.ShapeDtypeStruct((comps, full), jnp.float32),
            jax.ShapeDtypeStruct((full, wide), jnp.bfloat16),
        ],
        in_specs=[whole, whole],
        out_specs=[vmem, vmem],
        scratch_shapes=[
            pltpu.VMEM((parts, times, wide // parts), jnp.bfloat16),
            pltpu.VMEM((parts, comps, wide // parts), jnp.bfloat16),
            pltpu.SemaphoreType.DMA((2, parts)),
        ],
        compiler_params=params,
        name="response_terms",
    )(*(pltpu.with_memory_space_constraint(value[0], pltpu.HBM) for value in (data, maps)))
    square = pl.pallas_call(
        functools.partial(square_kernel, times),
        out_shape=jax.ShapeDtypeStruct((comps, full), jnp.float32),
        in_specs=[vmem],
        out_specs=vmem,
        compiler_params=params,
        cost_estimate=pl.CostEstimate(flops=6 * comps * comps * wide, bytes_accessed=full * wide * 2, transcendentals=0),
        name="square_terms",
    )(padded)

    def rows(value, at, size):
        return lax.dynamic_slice_in_dim(value, at * size, size, 0)

    def over_core(value):
        return swap(value, subj_step=0, vox_step=1)

    def over_side(value):
        return swap(value, subj_step=0, vox_step=2)

    quarter, eighth = half // 2, half // 4
    sums = rows(sums, core, half) + over_core(rows(sums, 1 - core, half))
    square = rows(square, core, half) + over_core(rows(square, 1 - core, half))

    bits = [1 << k for k in range(subjects.bit_length() - 1)]
    for bit in reversed(bits):
        size = sums.shape[0] // 2
        mine = jnp.where(s & bit > 0, 1, 0)
        sums = rows(sums, mine, size) + swap(rows(sums, 1 - mine, size), subj_step=bit, vox_step=0)
    sums = rows(sums, side, chunk) + over_side(rows(sums, 1 - side, chunk))
    step = 4
    while step < voxels:
        sums = sums + swap(sums, subj_step=0, vox_step=step)
        step *= 2
    sums = jnp.concatenate([sums, over_side(sums)], 0)
    for bit in bits[:-1]:
        sums = jnp.concatenate([sums, swap(sums, subj_step=bit, vox_step=0)], 0)
    responses = [sums, swap(sums, subj_step=bits[-1], vox_step=0)]

    square = rows(square, side, quarter) + over_side(rows(square, 1 - side, quarter))
    square = rows(square, level, eighth) + swap(rows(square, 1 - level, eighth), subj_step=0, vox_step=4)
    step = 8
    while step < voxels:
        square = square + swap(square, subj_step=0, vox_step=step)
        step *= 2
    square = jnp.concatenate([square, swap(square, subj_step=0, vox_step=4)], 0)
    squares = [square, over_side(square)]
    pieces = responses + squares
    pieces += [over_core(piece) for piece in pieces]

    response, new_maps = pl.pallas_call(
        functools.partial(finish_kernel, times, people, chunk),
        out_shape=[
            jax.ShapeDtypeStruct((times, comps), jnp.float32),
            jax.ShapeDtypeStruct((comps, wide), jnp.bfloat16),
        ],
        in_specs=[smem, vmem] + [vmem] * len(pieces),
        out_specs=[whole, whole],
        scratch_shapes=[
            pltpu.VMEM((comps, full), jnp.float32),
            pltpu.VMEM((comps, full), jnp.float32),
            pltpu.VMEM((times, comps), jnp.float32),
            pltpu.VMEM((parts, comps, wide // parts), jnp.bfloat16),
            pltpu.SemaphoreType.DMA((1 + parts,)),
        ],
        compiler_params=params,
        name="finish",
    )(place, padded, *pieces)
    return response, new_maps[None]


def solution(mesh):
    in_specs = (P("subj", None, "vox"), P("subj", None, "vox"))
    out_specs = (P(), P("subj", None, "vox"))
    return jax.shard_map(shards, mesh=mesh, in_specs=in_specs, out_specs=out_specs, check_vma=False)
```

```python
import functools

import jax
import jax.numpy as jnp
from jax import lax
from jax.experimental import pallas as pl
from jax.experimental.pallas import tpu as pltpu
from jax.sharding import PartitionSpec as P

TILE = 128
VMEM_LIMIT = 40 * 1024 * 1024
AXES = ("subj", "vox")
NT = (((1,), (1,)), ((), ()))


def dot(a, b):
    return jnp.dot(a, b, preferred_element_type=jnp.float32)


def dot_nt(a, b):
    return lax.dot_general(a, b, NT, preferred_element_type=jnp.float32)


def split(a):
    high = a.astype(jnp.bfloat16)
    return high, (a - high.astype(jnp.float32)).astype(jnp.bfloat16)


def dot3(a, b):
    (ah, al), (bh, bl) = split(a), split(b)
    rows = a.shape[0]
    product = dot(jnp.concatenate([ah, al], 0), bh)
    return product[:rows] + (product[rows:] + dot(ah, bl))


def grid_of(rows, cols):
    return (
        lax.broadcasted_iota(jnp.int32, (rows, cols), 0),
        lax.broadcasted_iota(jnp.int32, (rows, cols), 1),
    )


def response_kernel(times, data_ref, maps_ref, sums_ref, padded_ref, raw, weights, sems):
    parts, comps, part = weights.shape
    loads = []
    for k in range(parts):
        at = pl.ds(k * part, part)
        loads.append(pltpu.make_async_copy(data_ref.at[:, at], raw.at[k], sems.at[0, k]))
        loads.append(pltpu.make_async_copy(maps_ref.at[:, at], weights.at[k], sems.at[1, k]))
    for load in loads:
        load.start()
    full, wide = padded_ref.shape
    tail = times // 16 * 16
    padded_ref[tail:, :] = jnp.zeros((full - tail, wide), padded_ref.dtype)
    for k in range(parts):
        at = pl.ds(k * part, part)
        loads[2 * k].wait()
        loads[2 * k + 1].wait()
        padded_ref[0:times, at] = raw[k]
        term = dot_nt(weights[k], padded_ref[:, at])
        sums_ref[...] = term if k == 0 else sums_ref[...] + term


def square_kernel(times, padded_ref, square_ref):
    comps = square_ref.shape[0]
    upper = dot_nt(padded_ref[0:comps, :], padded_ref[...])
    lower = dot_nt(padded_ref[comps:, :], padded_ref[comps:, :])
    row, col = grid_of(comps, comps)
    diagonal = jnp.sum(jnp.where(row == col, lower, 0.0), axis=1, keepdims=True)
    square_ref[:, 0:comps] = jnp.where(col >= row, upper[:, 0:comps], lower)
    square_ref[:, comps:] = jnp.where(col == times - comps, diagonal, upper[:, comps:])


def dot2(a, high, low):
    return dot(a, high) + dot(a, low)


def gram_terms(signal, high_ref, low_ref):
    comps = high_ref.shape[1]
    first, second = signal[:, 0:comps], signal[:, comps:]
    left = dot2(first, high_ref[0], low_ref[0])
    right = dot2(first, high_ref[1], low_ref[1]) + dot2(second, high_ref[2], low_ref[2])
    return left, right


def unpack_kernel(times, people, chunk, place_ref, *refs):
    pieces, own, (high_ref, low_ref, terms_ref, packed, mine) = refs[:4], refs[4:6], refs[6:]
    comps, full = packed.shape
    half = comps // 2
    quarter, eighth = half // 2, half // 4
    core, spot, side, level = place_ref[0], place_ref[1], place_ref[2], place_ref[3]
    for which, parts in ((core, pieces[0:2]), (1 - core, pieces[2:4])):
        for d in range(4):
            at = which * half + (side ^ (d >> 1)) * quarter + (level ^ (d & 1)) * eighth
            piece = parts[d >> 1][(d & 1) * eighth : (d & 1) * eighth + eighth, :]
            packed[pl.ds(pl.multiple_of(at, 8), eighth), :] = piece
    for d in range(half // chunk):
        piece = own[d * chunk // quarter][d * chunk % quarter : d * chunk % quarter + chunk, :]
        mine[pl.ds(pl.multiple_of((spot ^ d) * chunk, 8), chunk), :] = piece
    row, col = grid_of(comps, comps)
    corner, beside = packed[:, 0:comps], packed[:, comps:]
    last = jnp.sum(jnp.where(col == times - comps, beside, 0.0), axis=1, keepdims=True)
    u11 = jnp.where(col > row, corner, jnp.where(col == row, 0.5 * corner, 0.0))
    u22 = jnp.where(col < row, corner, jnp.where(col == row, 0.5 * last, 0.0))
    u12 = jnp.where(col < times - comps, beside, 0.0)
    for k, part in enumerate((u11, u12, u22)):
        high_ref[k], low_ref[k] = split(part)
    signal = (mine[...] / people).astype(jnp.bfloat16)
    terms_ref[:, 0:comps], terms_ref[:, comps:] = gram_terms(signal, high_ref, low_ref)


def finish_kernel(times, people, chunk, place_ref, data_ref, high_ref, low_ref, terms_ref, *refs):
    pieces, (response_ref, maps_ref, total, terms, turned, new, sems) = refs[:4], refs[4:]
    comps, full = total.shape
    half, block = comps // 2, full // 2
    quarter = half // 2
    core, spot = place_ref[0], place_ref[1]
    for which, parts in ((core, pieces[0:2]), (1 - core, pieces[2:4])):
        for d in range(half // chunk):
            at = which * half + (spot ^ d) * chunk
            piece = parts[d * chunk // quarter][d * chunk % quarter : d * chunk % quarter + chunk, :]
            total[pl.ds(pl.multiple_of(at, 8), chunk), :] = piece
    mine, theirs = pl.multiple_of(core * half, 8), pl.multiple_of((1 - core) * half, 8)
    terms[pl.ds(mine, half), :] = terms_ref[...]
    signal = (total[pl.ds(theirs, half), :] / people).astype(jnp.bfloat16)
    left, right = gram_terms(signal, high_ref, low_ref)
    terms[pl.ds(theirs, half), 0:block] = left
    terms[pl.ds(theirs, half), block:] = right
    response = total[...] / people

    def turn(k):
        size = min(times - k * TILE, TILE)
        turned[k * TILE : k * TILE + size, :] = response[:, k * TILE : (k + 1) * TILE].T[0:size, :]

    signal = response.astype(jnp.bfloat16)
    first, second = signal[:, 0:block], signal[:, block:]
    left, right = terms[:, 0:block], terms[:, block:]
    lh, ll = split(left)
    rh, rl = split(right)
    product = (dot_nt(lh, first) + dot_nt(ll, first)) + (dot_nt(rh, second) + dot_nt(rl, second))
    gram = product + product.T
    scale = jnp.sqrt(jnp.sum(gram * gram) + 1e-06)
    row, col = grid_of(comps, comps)
    diagonal = jnp.where(row == col, 1.0, 0.0)

    def two_steps(t, t2):
        inner = 1.6875 * diagonal - 0.5625 * t + 0.0625 * t2
        return 2.25 * diagonal - 2.4375 * t + dot3(t2, inner)

    t = gram / scale
    t2 = dot3(t, t)
    turn(0)
    first_two = two_steps(t, t2)
    turn(1)
    t = dot3(dot3(t, first_two), first_two)
    turn(2)
    t2 = dot3(t, t)
    moved = dot3(first_two, t)
    next_two = two_steps(t, t2)
    turn(3)
    inverse = dot3(first_two, next_two)
    moved = dot3(moved, next_two)
    cubed = dot3(next_two, next_two)
    answer = pltpu.make_async_copy(turned, response_ref, sems.at[0])
    answer.start()
    inverse = 1.5 * inverse - 0.5 * dot3(moved, cubed)
    factor = inverse / jnp.sqrt(scale)
    fh, fl = split(factor)
    weights = dot(fh, signal) + dot(fl, signal)
    both = jnp.concatenate(split(weights), 0)
    stores = []
    part = new.shape[2]
    for k in range(new.shape[0]):
        at = pl.ds(k * part, part)
        result = dot(both, data_ref[:, at])
        new[k] = (result[0:comps] + result[comps:]).astype(jnp.bfloat16)
        stores.append(pltpu.make_async_copy(new.at[k], maps_ref.at[:, at], sems.at[1 + k]))
        stores[-1].start()
    for store in [answer, *stores]:
        store.wait()


def exchange(value, subjects, voxels, subj_step, vox_step):
    pairs = [
        (s * voxels + v, (s ^ subj_step) * voxels + (v ^ vox_step))
        for s in range(subjects)
        for v in range(voxels)
    ]
    return lax.ppermute(value, AXES, pairs)


def shards(data, maps):
    subjects, voxels = lax.axis_size("subj"), lax.axis_size("vox")
    _, times, wide = data.shape
    comps = maps.shape[1]
    people = subjects * data.shape[0]
    full, half = 2 * comps, comps // 2
    spots = 2 * subjects
    chunk = half // spots
    swap = functools.partial(exchange, subjects=subjects, voxels=voxels)
    s, v = lax.axis_index("subj"), lax.axis_index("vox")
    core, side = v & 1, (v >> 1) & 1
    spot, level = s * 2 + side, (v >> 2) & 1
    place = jnp.stack([core, spot, side, level]).astype(jnp.int32)
    smem = pl.BlockSpec(memory_space=pltpu.SMEM)
    vmem = pl.BlockSpec(memory_space=pltpu.VMEM)
    params = pltpu.CompilerParams(vmem_limit_bytes=VMEM_LIMIT)

    whole = pl.BlockSpec(memory_space=pltpu.HBM)
    parts = 2 if wide % 512 == 0 else 1
    sums, padded = pl.pallas_call(
        functools.partial(response_kernel, times),
        out_shape=[
            jax.ShapeDtypeStruct((comps, full), jnp.float32),
            jax.ShapeDtypeStruct((full, wide), jnp.bfloat16),
        ],
        in_specs=[whole, whole],
        out_specs=[vmem, vmem],
        scratch_shapes=[
            pltpu.VMEM((parts, times, wide // parts), jnp.bfloat16),
            pltpu.VMEM((parts, comps, wide // parts), jnp.bfloat16),
            pltpu.SemaphoreType.DMA((2, parts)),
        ],
        compiler_params=params,
        name="response_terms",
    )(*(pltpu.with_memory_space_constraint(value[0], pltpu.HBM) for value in (data, maps)))
    square = pl.pallas_call(
        functools.partial(square_kernel, times),
        out_shape=jax.ShapeDtypeStruct((comps, full), jnp.float32),
        in_specs=[vmem],
        out_specs=vmem,
        compiler_params=params,
        cost_estimate=pl.CostEstimate(flops=6 * comps * comps * wide, bytes_accessed=full * wide * 2, transcendentals=0),
        name="square_terms",
    )(padded)

    def rows(value, at, size):
        return lax.dynamic_slice_in_dim(value, at * size, size, 0)

    def over_core(value):
        return swap(value, subj_step=0, vox_step=1)

    def over_side(value):
        return swap(value, subj_step=0, vox_step=2)

    quarter, eighth = half // 2, half // 4
    sums = rows(sums, core, half) + over_core(rows(sums, 1 - core, half))
    square = rows(square, core, half) + over_core(rows(square, 1 - core, half))

    bits = [1 << k for k in range(subjects.bit_length() - 1)]
    for bit in reversed(bits):
        size = sums.shape[0] // 2
        mine = jnp.where(s & bit > 0, 1, 0)
        sums = rows(sums, mine, size) + swap(rows(sums, 1 - mine, size), subj_step=bit, vox_step=0)
    sums = rows(sums, side, chunk) + over_side(rows(sums, 1 - side, chunk))
    step = 4
    while step < voxels:
        sums = sums + swap(sums, subj_step=0, vox_step=step)
        step *= 2
    sums = jnp.concatenate([sums, over_side(sums)], 0)
    for bit in bits[:-1]:
        sums = jnp.concatenate([sums, swap(sums, subj_step=bit, vox_step=0)], 0)
    responses = [sums, swap(sums, subj_step=bits[-1], vox_step=0)]

    square = rows(square, side, quarter) + over_side(rows(square, 1 - side, quarter))
    square = rows(square, level, eighth) + swap(rows(square, 1 - level, eighth), subj_step=0, vox_step=4)
    step = 8
    while step < voxels:
        square = square + swap(square, subj_step=0, vox_step=step)
        step *= 2
    square = jnp.concatenate([square, swap(square, subj_step=0, vox_step=4)], 0)
    squares = [square, over_side(square)]
    own = list(responses)
    responses += [over_core(piece) for piece in responses]
    squares += [over_core(piece) for piece in squares]
    halves = pl.pallas_call(
        functools.partial(unpack_kernel, times, people, chunk),
        out_shape=[jax.ShapeDtypeStruct((3, comps, comps), jnp.bfloat16)] * 2
        + [jax.ShapeDtypeStruct((half, full), jnp.float32)],
        in_specs=[smem] + [vmem] * (len(squares) + 2),
        out_specs=[vmem] * 3,
        scratch_shapes=[pltpu.VMEM((comps, full), jnp.float32), pltpu.VMEM((half, full), jnp.float32)],
        compiler_params=params,
        name="unpack",
    )(place, *squares, *own)

    response, new_maps = pl.pallas_call(
        functools.partial(finish_kernel, times, people, chunk),
        out_shape=[
            jax.ShapeDtypeStruct((times, comps), jnp.float32),
            jax.ShapeDtypeStruct((comps, wide), jnp.bfloat16),
        ],
        in_specs=[smem] + [vmem] * (4 + len(responses)),
        out_specs=[whole, whole],
        scratch_shapes=[
            pltpu.VMEM((comps, full), jnp.float32),
            pltpu.VMEM((comps, full), jnp.float32),
            pltpu.VMEM((times, comps), jnp.float32),
            pltpu.VMEM((parts, comps, wide // parts), jnp.bfloat16),
            pltpu.SemaphoreType.DMA((1 + parts,)),
        ],
        compiler_params=params,
        name="finish",
    )(place, padded, *halves, *responses)
    return response, new_maps[None]


def solution(mesh):
    in_specs = (P("subj", None, "vox"), P("subj", None, "vox"))
    out_specs = (P(), P("subj", None, "vox"))
    return jax.shard_map(shards, mesh=mesh, in_specs=in_specs, out_specs=out_specs, check_vma=False)
```

```python
import functools

import jax
import jax.numpy as jnp
from jax import lax
from jax.experimental import pallas as pl
from jax.experimental.pallas import tpu as pltpu
from jax.sharding import PartitionSpec as P

TILE = 128
VMEM_LIMIT = 40 * 1024 * 1024
AXES = ("subj", "vox")
NT = (((1,), (1,)), ((), ()))


def dot(a, b):
    return jnp.dot(a, b, preferred_element_type=jnp.float32)


def dot_nt(a, b):
    return lax.dot_general(a, b, NT, preferred_element_type=jnp.float32)


def split(a):
    high = a.astype(jnp.bfloat16)
    return high, (a - high.astype(jnp.float32)).astype(jnp.bfloat16)


def dot3(a, b):
    (ah, al), (bh, bl) = split(a), split(b)
    rows = a.shape[0]
    product = dot(jnp.concatenate([ah, al], 0), bh)
    return product[:rows] + (product[rows:] + dot(ah, bl))


def grid_of(rows, cols):
    return (
        lax.broadcasted_iota(jnp.int32, (rows, cols), 0),
        lax.broadcasted_iota(jnp.int32, (rows, cols), 1),
    )


def response_kernel(times, data_ref, maps_ref, sums_ref, padded_ref, raw, weights, sems):
    parts, comps, part = weights.shape
    loads = []
    for k in range(parts):
        at = pl.ds(k * part, part)
        loads.append(pltpu.make_async_copy(data_ref.at[:, at], raw.at[k], sems.at[0, k]))
        loads.append(pltpu.make_async_copy(maps_ref.at[:, at], weights.at[k], sems.at[1, k]))
    for load in loads:
        load.start()
    full, wide = padded_ref.shape
    tail = times // 16 * 16
    padded_ref[tail:, :] = jnp.zeros((full - tail, wide), padded_ref.dtype)
    for k in range(parts):
        at = pl.ds(k * part, part)
        loads[2 * k].wait()
        loads[2 * k + 1].wait()
        padded_ref[0:times, at] = raw[k]
        term = dot_nt(weights[k], padded_ref[:, at])
        sums_ref[...] = term if k == 0 else sums_ref[...] + term


def square_kernel(times, padded_ref, square_ref):
    comps = square_ref.shape[0]
    upper = dot_nt(padded_ref[0:comps, :], padded_ref[...])
    lower = dot_nt(padded_ref[comps:, :], padded_ref[comps:, :])
    row, col = grid_of(comps, comps)
    diagonal = jnp.sum(jnp.where(row == col, lower, 0.0), axis=1, keepdims=True)
    square_ref[:, 0:comps] = jnp.where(col >= row, upper[:, 0:comps], lower)
    square_ref[:, comps:] = jnp.where(col == times - comps, diagonal, upper[:, comps:])


def finish_kernel(times, people, chunk, place_ref, data_ref, *refs):
    pieces, (response_ref, maps_ref, total, packed, turned, new, sems) = refs[:8], refs[8:]
    comps, full = total.shape
    half, block = comps // 2, full // 2
    quarter, eighth = half // 2, half // 4
    core, spot, side, level = place_ref[0], place_ref[1], place_ref[2], place_ref[3]
    for which, parts in ((core, pieces[0:4]), (1 - core, pieces[4:8])):
        for d in range(half // chunk):
            at = which * half + (spot ^ d) * chunk
            piece = parts[d * chunk // quarter][d * chunk % quarter : d * chunk % quarter + chunk, :]
            total[pl.ds(pl.multiple_of(at, 8), chunk), :] = piece
        for d in range(4):
            at = which * half + (side ^ (d >> 1)) * quarter + (level ^ (d & 1)) * eighth
            piece = parts[2 + (d >> 1)][(d & 1) * eighth : (d & 1) * eighth + eighth, :]
            packed[pl.ds(pl.multiple_of(at, 8), eighth), :] = piece
    response = total[...] / people

    def turn(k):
        size = min(times - k * TILE, TILE)
        turned[k * TILE : k * TILE + size, :] = response[:, k * TILE : (k + 1) * TILE].T[0:size, :]

    signal = response.astype(jnp.bfloat16)
    first, second = signal[:, 0:block], signal[:, block:]
    row, col = grid_of(comps, block)
    corner = packed[:, 0:block]
    beside = packed[:, block:]
    last = jnp.sum(jnp.where(col == times - block, beside, 0.0), axis=1, keepdims=True)
    u11 = jnp.where(col > row, corner, jnp.where(col == row, 0.5 * corner, 0.0))
    u22 = jnp.where(col < row, corner, jnp.where(col == row, 0.5 * last, 0.0))
    u12 = jnp.where(col < times - block, beside, 0.0)

    def dot2(a, b):
        high, low = split(b)
        return dot(a, high) + dot(a, low)

    left = dot2(first, u11)
    right = dot2(first, u12) + dot2(second, u22)
    lh, ll = split(left)
    rh, rl = split(right)
    product = (dot_nt(lh, first) + dot_nt(ll, first)) + (dot_nt(rh, second) + dot_nt(rl, second))
    gram = product + product.T
    scale = jnp.sqrt(jnp.sum(gram * gram) + 1e-06)
    row, col = grid_of(comps, comps)
    diagonal = jnp.where(row == col, 1.0, 0.0)

    def two_steps(t, t2):
        inner = 1.6875 * diagonal - 0.5625 * t + 0.0625 * t2
        return 2.25 * diagonal - 2.4375 * t + dot3(t2, inner)

    t = gram * (1.0 / scale)
    t2 = dot3(t, t)
    turn(0)
    first_two = two_steps(t, t2)
    turn(1)
    t = dot3(dot3(t, first_two), first_two)
    turn(2)
    t2 = dot3(t, t)
    moved = dot3(first_two, t)
    next_two = two_steps(t, t2)
    turn(3)
    inverse = dot3(first_two, next_two)
    moved = dot3(moved, next_two)
    cubed = dot3(next_two, next_two)
    answer = pltpu.make_async_copy(turned, response_ref, sems.at[0])
    answer.start()
    inverse = 1.5 * inverse - 0.5 * dot3(moved, cubed)
    factor = inverse * (1.0 / jnp.sqrt(scale))
    fh, fl = split(factor)
    weights = dot(fh, signal) + dot(fl, signal)
    both = jnp.concatenate(split(weights), 0)
    stores = []
    part = new.shape[2]
    for k in range(new.shape[0]):
        at = pl.ds(k * part, part)
        result = dot(both, data_ref[:, at])
        new[k] = (result[0:comps] + result[comps:]).astype(jnp.bfloat16)
        stores.append(pltpu.make_async_copy(new.at[k], maps_ref.at[:, at], sems.at[1 + k]))
        stores[-1].start()
    for store in [answer, *stores]:
        store.wait()


def exchange(value, subjects, voxels, subj_step, vox_step):
    pairs = [
        (s * voxels + v, (s ^ subj_step) * voxels + (v ^ vox_step))
        for s in range(subjects)
        for v in range(voxels)
    ]
    return lax.ppermute(value, AXES, pairs)


def shards(data, maps):
    subjects, voxels = lax.axis_size("subj"), lax.axis_size("vox")
    _, times, wide = data.shape
    comps = maps.shape[1]
    people = subjects * data.shape[0]
    full, half = 2 * comps, comps // 2
    spots = 2 * subjects
    chunk = half // spots
    swap = functools.partial(exchange, subjects=subjects, voxels=voxels)
    s, v = lax.axis_index("subj"), lax.axis_index("vox")
    core, side = v & 1, (v >> 1) & 1
    spot, level = s * 2 + side, (v >> 2) & 1
    place = jnp.stack([core, spot, side, level]).astype(jnp.int32)
    smem = pl.BlockSpec(memory_space=pltpu.SMEM)
    vmem = pl.BlockSpec(memory_space=pltpu.VMEM)
    params = pltpu.CompilerParams(vmem_limit_bytes=VMEM_LIMIT)

    whole = pl.BlockSpec(memory_space=pltpu.HBM)
    parts = 2 if wide % 512 == 0 else 1
    sums, padded = pl.pallas_call(
        functools.partial(response_kernel, times),
        out_shape=[
            jax.ShapeDtypeStruct((comps, full), jnp.float32),
            jax.ShapeDtypeStruct((full, wide), jnp.bfloat16),
        ],
        in_specs=[whole, whole],
        out_specs=[vmem, vmem],
        scratch_shapes=[
            pltpu.VMEM((parts, times, wide // parts), jnp.bfloat16),
            pltpu.VMEM((parts, comps, wide // parts), jnp.bfloat16),
            pltpu.SemaphoreType.DMA((2, parts)),
        ],
        compiler_params=params,
        name="response_terms",
    )(*(pltpu.with_memory_space_constraint(value[0], pltpu.HBM) for value in (data, maps)))
    square = pl.pallas_call(
        functools.partial(square_kernel, times),
        out_shape=jax.ShapeDtypeStruct((comps, full), jnp.float32),
        in_specs=[vmem],
        out_specs=vmem,
        compiler_params=params,
        cost_estimate=pl.CostEstimate(flops=6 * comps * comps * wide, bytes_accessed=full * wide * 2, transcendentals=0),
        name="square_terms",
    )(padded)

    def rows(value, at, size):
        return lax.dynamic_slice_in_dim(value, at * size, size, 0)

    def over_core(value):
        return swap(value, subj_step=0, vox_step=1)

    def over_side(value):
        return swap(value, subj_step=0, vox_step=2)

    quarter, eighth = half // 2, half // 4
    sums = rows(sums, core, half) + over_core(rows(sums, 1 - core, half))
    square = rows(square, core, half) + over_core(rows(square, 1 - core, half))

    bits = [1 << k for k in range(subjects.bit_length() - 1)]
    for bit in reversed(bits):
        size = sums.shape[0] // 2
        mine = jnp.where(s & bit > 0, 1, 0)
        sums = rows(sums, mine, size) + swap(rows(sums, 1 - mine, size), subj_step=bit, vox_step=0)
    sums = rows(sums, side, chunk) + over_side(rows(sums, 1 - side, chunk))
    step = 4
    while step < voxels:
        sums = sums + swap(sums, subj_step=0, vox_step=step)
        step *= 2
    sums = jnp.concatenate([sums, over_side(sums)], 0)
    for bit in bits[:-1]:
        sums = jnp.concatenate([sums, swap(sums, subj_step=bit, vox_step=0)], 0)
    responses = [sums, swap(sums, subj_step=bits[-1], vox_step=0)]

    square = rows(square, side, quarter) + over_side(rows(square, 1 - side, quarter))
    square = rows(square, level, eighth) + swap(rows(square, 1 - level, eighth), subj_step=0, vox_step=4)
    step = 8
    while step < voxels:
        square = square + swap(square, subj_step=0, vox_step=step)
        step *= 2
    square = jnp.concatenate([square, swap(square, subj_step=0, vox_step=4)], 0)
    squares = [square, over_side(square)]
    pieces = responses + squares
    pieces += [over_core(piece) for piece in pieces]

    response, new_maps = pl.pallas_call(
        functools.partial(finish_kernel, times, people, chunk),
        out_shape=[
            jax.ShapeDtypeStruct((times, comps), jnp.float32),
            jax.ShapeDtypeStruct((comps, wide), jnp.bfloat16),
        ],
        in_specs=[smem, vmem] + [vmem] * len(pieces),
        out_specs=[whole, whole],
        scratch_shapes=[
            pltpu.VMEM((comps, full), jnp.float32),
            pltpu.VMEM((comps, full), jnp.float32),
            pltpu.VMEM((times, comps), jnp.float32),
            pltpu.VMEM((parts, comps, wide // parts), jnp.bfloat16),
            pltpu.SemaphoreType.DMA((1 + parts,)),
        ],
        compiler_params=params,
        name="finish",
    )(place, padded, *pieces)
    return response, new_maps[None]


def solution(mesh):
    in_specs = (P("subj", None, "vox"), P("subj", None, "vox"))
    out_specs = (P(), P("subj", None, "vox"))
    return jax.shard_map(shards, mesh=mesh, in_specs=in_specs, out_specs=out_specs, check_vma=False)
```
